32 devices in a mesh: req: 16 (over z, x, core), tp: 2 (over y).
Axes of the slice: x: 2, y: 2, z: 4, core: 2. Of those that a mesh axis runs over, the one named last changes fastest.
Arguments:
- suffix_query: bfloat16 [4096, 5120], P('req', 'tp')
- suffix_key: bfloat16 [4096, 1024], P('req', 'tp')
- suffix_value: bfloat16 [4096, 1024], P('req', 'tp'), may hold values from -6 to 6
- prefix_key: bfloat16 [16, 1024, 1024], P('req', None, 'tp')
- prefix_value: bfloat16 [16, 1024, 1024], P('req', None, 'tp'), may hold values from -6 to 6
- residual: bfloat16 [4096, 5120], P('req'), may hold values from -6 to 6
- out_weight: bfloat16 [5120, 5120], P('tp'), may hold values from -0.15625 to 0.15625
- norm_gain: bfloat16 [5120], P('tp'), may hold values from 0.099609375 to 1.8984375
- lengths: int32 [16], replicated, may hold values from 1 to 256, 2457 in all
- request_slot: int32 [16], replicated, may hold values from 0 to 15, each once
- prefix_owner: int32 [16], replicated, may hold values from 0 to 15, each once
- request_group: int32 [16, 1], replicated, may hold values from 0 to 3
Outputs:
- hidden: bfloat16 [4096, 5120], P('req', 'tp')
- normed: bfloat16 [4096, 5120], P('req', 'tp')
- cache_key: bfloat16 [4096, 1024], P('req', 'tp')
The draws below stay inside these ranges and needn't reach their ends.
Inputs may be any that keep to these rules, and one draw needn't show every extreme that they name: `request_slot`: a permutation. `prefix_owner`: a permutation. `request_group`: every group has one request or more. `lengths`: some request has all 256 slots live.
All inputs are finite; a program needn't handle non-finite values.
Results may differ from the reference program's by a relative error of at most 0.0067.
Values may be sent and summed in bfloat16 or wider, within the bound.
A program may use at most 128 MiB of HBM per device.

```python
import math
import jax
import jax.numpy as jnp
import numpy as np
from jax import lax

D = 5120
QH = 40
KVH = 8
HD = 128
GROUPS = 4
SLOTS = 256
PBLK = 1024
REQS = 16
PREFIX = 4096
ROWS = 4096
N_REQ = 16


def draw_prefix_key(key, part):
    noise = jax.random.normal(jax.random.fold_in(key, 1), (N_REQ, PBLK, KVH * HD), jnp.float32)
    values = noise
    return jnp.clip(values, -6.0, 6.0).astype(jnp.bfloat16)


def draw_suffix_key(key, part):
    noise = jax.random.normal(jax.random.fold_in(key, 5), (N_REQ * SLOTS, KVH * HD), jnp.float32)
    values = 1.4 * noise
    return jnp.clip(values, -8.0, 8.0).astype(jnp.bfloat16)


def draw_suffix_query(key, part):
    noise = jax.random.normal(jax.random.fold_in(key, 3), (N_REQ * SLOTS, QH * HD), jnp.float32)
    values = 3.0 * noise
    return jnp.clip(values, -12.0, 12.0).astype(jnp.bfloat16)


def shard_levels(own_key, shape, cuts, least, top_value):
    level, own = 1.0, jax.random.fold_in(own_key, 6)
    for dim, shards_of in cuts:
        steps = jnp.exp(jax.random.uniform(jax.random.fold_in(own, dim), (shards_of,), jnp.float32, least / len(cuts), top_value / len(cuts)))
        level = level * jnp.repeat(steps, shape[dim] // shards_of).reshape([-1 if axis == dim else 1 for axis in range(len(shape))])
    return level


def different_ones(key, rows, amount, top, lift):
    order = jax.random.permutation(jax.random.fold_in(key, 1), amount)
    favour = order
    for power in range(3):
        favour = favour * favour // amount
    favour = favour * lift // amount
    lots = jax.random.randint(jax.random.fold_in(key, 2), (rows, amount), 0, 4096) + favour
    sure = jax.random.permutation(jax.random.fold_in(key, 3), rows)[jnp.arange(amount) % rows]
    lots = jnp.where(jnp.arange(rows)[:, None] == sure[None, :], 1 << 14, lots)
    merit = lots * amount + jnp.arange(amount)
    return lax.top_k(merit.astype(jnp.int32), top)[1].astype(jnp.int32)


def profile(amount, total, limit, slope):
    portions = [(1 << 20) // math.isqrt(rank ** slope) + 1 for rank in range(2, amount + 1)]
    surplus, given = total - limit - (amount - 1), [1] * (amount - 1)
    while surplus > 0:
        free = [i for i in range(amount - 1) if given[i] < limit]
        mass, left = sum([portions[i] for i in free]), surplus
        for i in free:
            addition = min(limit - given[i], max(1, left * portions[i] // mass), surplus)
            given[i] = given[i] + addition
            surplus = surplus - addition
    return np.array([limit] + given)


def ragged_sizes(own_key, amount, total, limit, lean):
    if amount == 2:
        one = jax.random.randint(own_key, (), max(1, total - limit), min(limit, total - 1) + 1)
        return jnp.stack([one, total - one])
    sizes = jnp.asarray(profile(amount, total, limit, lean), jnp.int32)
    couples = (amount - 1) // 2
    source_of, taker = sizes[1:1 + 2 * couples:2], sizes[2:2 + 2 * couples:2]
    margin = jnp.minimum(source_of - 1, limit - taker)
    moved = jax.random.randint(jax.random.fold_in(own_key, 1), (couples,), 0, 1 << 20) % (margin + 1)
    sizes = sizes.at[1:1 + 2 * couples:2].set(source_of - moved).at[2:2 + 2 * couples:2].set(taker + moved)
    return sizes[jax.random.permutation(jax.random.fold_in(own_key, 2), amount)]


def scatter_about(own_key, shape, deviation, bound, pieces=(), dtype=jnp.bfloat16):
    factor_of = shard_levels(own_key, shape, pieces, -0.22, 0.18) if pieces else 1.0
    array = jax.random.normal(own_key, shape, jnp.float32) * deviation * factor_of
    return jnp.minimum(jnp.maximum(array, -bound), bound).astype(dtype)


def setup_inputs(seed: int = 0) -> dict:
    key_list = jax.random.split(jax.random.key(seed), 13)
    suffix_query = draw_suffix_query(jax.random.fold_in(key_list[12], 71), 0)
    suffix_key = draw_suffix_key(jax.random.fold_in(key_list[12], 71), 0)
    suffix_value = scatter_about(key_list[2], (ROWS, KVH * HD), 1.0, 6.0, ((0, 16), (1, 2)))
    prefix_key = draw_prefix_key(jax.random.fold_in(key_list[12], 71), 0)
    prefix_value = scatter_about(key_list[4], (N_REQ, PBLK, KVH * HD), 1.0, 6.0, ((0, 16), (2, 2)))
    residual = scatter_about(key_list[5], (ROWS, D), 1.0, 6.0, ((0, 16),))
    out_weight = scatter_about(key_list[6], (QH * HD, D), (QH * HD // 4) ** -0.5, 0.15625, ((0, 2),))
    norm_gain = jnp.clip(1.0 + 0.18 * jax.random.normal(key_list[7], (D,), jnp.float32), 0.099609375, 1.8984375).astype(jnp.bfloat16)
    lengths = ragged_sizes(key_list[8], REQS, REQS * SLOTS * 3 // 5, SLOTS, 2).astype(jnp.int32)
    request_slot = jax.random.permutation(key_list[9], N_REQ).astype(jnp.int32)
    prefix_owner = jax.random.permutation(key_list[10], N_REQ).astype(jnp.int32)
    request_group = different_ones(key_list[11], REQS, GROUPS, 1, 4096)
    return {"suffix_query": suffix_query, "suffix_key": suffix_key, "suffix_value": suffix_value, "prefix_key": prefix_key, "prefix_value": prefix_value, "residual": residual, "out_weight": out_weight, "norm_gain": norm_gain, "lengths": lengths, "request_slot": request_slot, "prefix_owner": prefix_owner, "request_group": request_group}


THETA = 1000000.0
NEGATIVE = -1e+30
EPSILON = 1e-06

def rotate(values, head_count, position_base):
    row_count = values.shape[0]
    half_dim = HD // 2
    positions = (position_base + jnp.arange(row_count)).astype(jnp.float32)
    frequency = THETA ** (-(jnp.arange(half_dim).astype(jnp.float32) * 2.0 / HD))
    angles = positions[:, None] * frequency[None, :]
    cosines = jnp.cos(angles)[:, None, :]
    sines = jnp.sin(angles)[:, None, :]
    per_head = values.reshape(row_count, head_count, HD)
    front_half = per_head[..., :half_dim]
    back_half = per_head[..., half_dim:]
    joined = jnp.concatenate([front_half * cosines - back_half * sines, back_half * cosines + front_half * sines], axis=-1)
    return joined.reshape(row_count, head_count * HD)

def attend(queries, keys_in, values_in, visible):
    row_count = queries.shape[0]
    kv_count = keys_in.shape[-1] // HD
    ratio = queries.shape[1] // HD // kv_count
    query_heads = queries.reshape(row_count, kv_count, ratio, HD).astype(jnp.float32)
    key_heads = keys_in.reshape(-1, kv_count, HD).astype(jnp.float32)
    value_heads = values_in.reshape(-1, kv_count, HD).astype(jnp.float32)
    scores = jnp.einsum('sgrd,kgd->sgrk', query_heads, key_heads) * HD ** (-0.5)
    if visible is not None:
        scores = jnp.where(visible[:, None, None, :], scores, NEGATIVE)
    block_max = lax.optimization_barrier(jnp.max(scores, axis=-1))
    weights = jnp.exp(scores - block_max[..., None])
    block_sum = lax.optimization_barrier(jnp.sum(weights, axis=-1))
    probs = weights.astype(jnp.bfloat16).astype(jnp.float32)
    block_out = jnp.einsum('sgrk,kgd->sgrd', probs, value_heads) / block_sum[..., None]
    heads = kv_count * ratio
    return (block_max.reshape(row_count, heads), block_sum.reshape(row_count, heads), block_out.reshape(row_count, heads, HD))

def reference(suffix_query, suffix_key, suffix_value, prefix_key, prefix_value, residual, out_weight, norm_gain, lengths, request_slot, prefix_owner, request_group):
    per_group = N_REQ // GROUPS
    owner_table = prefix_owner.reshape(GROUPS, per_group)
    positions = jnp.arange(SLOTS).astype(jnp.int32)

    def one_request(place):
        request = request_slot[place]
        group_now = request_group[request, 0]
        length_now = lengths[request]
        first_row = (place * SLOTS).astype(jnp.int32)
        query_rows = lax.dynamic_slice_in_dim(suffix_query, first_row, SLOTS, 0)
        key_rows = lax.dynamic_slice_in_dim(suffix_key, first_row, SLOTS, 0)
        value_rows = lax.dynamic_slice_in_dim(suffix_value, first_row, SLOTS, 0)
        queries = rotate(query_rows.astype(jnp.float32), QH, PREFIX).astype(jnp.bfloat16)
        keys_rot = rotate(key_rows.astype(jnp.float32), KVH, PREFIX)
        live_rows = positions < length_now
        cache_rows = jnp.where(live_rows[:, None], keys_rot, 0.0).astype(jnp.bfloat16)
        visible = (positions[None, :] <= positions[:, None]) & (positions[None, :] < length_now)
        own_max, own_sum, own_out = attend(queries, cache_rows, value_rows, visible)
        blocks = owner_table[group_now]

        def one_block(device):
            part_max, part_sum, part_out = attend(queries, prefix_key[device], prefix_value[device], None)
            rounded = lax.optimization_barrier(part_out.astype(jnp.bfloat16)).astype(jnp.float32)
            return (part_max, part_sum, rounded)
        part_maxes, part_sums, part_outs = lax.map(one_block, blocks)
        overall = jnp.maximum(own_max, lax.optimization_barrier(jnp.max(part_maxes, axis=0)))
        own_weight = own_sum * jnp.exp(own_max - overall)
        part_weights = part_sums * jnp.exp(part_maxes - overall[None])
        numerator = own_weight[..., None] * own_out + lax.optimization_barrier(jnp.sum(part_weights[..., None] * part_outs, axis=0))
        denominator = own_weight + lax.optimization_barrier(jnp.sum(part_weights, axis=0))
        mixed = jnp.where(live_rows[:, None, None], numerator / denominator[..., None], 0.0)
        return (mixed.astype(jnp.bfloat16).reshape(SLOTS, QH * HD), cache_rows)
    attn, cache_rows = lax.map(one_request, jnp.arange(N_REQ).astype(jnp.int32))
    attn = attn.reshape(N_REQ * SLOTS, QH * HD)
    cache_key = cache_rows.reshape(N_REQ * SLOTS, KVH * HD)
    hidden = (residual.astype(jnp.float32) + jnp.dot(attn, out_weight, preferred_element_type=jnp.float32)).astype(jnp.bfloat16)
    widened = hidden.astype(jnp.float32)
    scale_rows = lax.rsqrt(lax.optimization_barrier(jnp.mean(widened * widened, axis=1, keepdims=True)) + EPSILON)
    normed = (widened * scale_rows * norm_gain.astype(jnp.float32)[None, :]).astype(jnp.bfloat16)
    return (hidden, normed, cache_key)
```

```python
import functools

import jax
import jax.numpy as jnp
from jax import lax
from jax.experimental import pallas as pl
from jax.experimental.pallas import tpu as pltpu
from jax.sharding import PartitionSpec as P

HD = 128
GROUPS = 4

THETA = 1000000.0
NEGATIVE = -1e30
EPSILON = 1e-06
LOG2E = 1.4426950408889634


def rope_tables(row_count, position_base):
    half_dim = HD // 2
    positions = (position_base + jnp.arange(row_count)).astype(jnp.float32)
    frequency = THETA ** (-(jnp.arange(half_dim).astype(jnp.float32) * 2.0 / HD))
    angles = positions[:, None] * frequency[None, :]
    cosines, sines = jnp.cos(angles), jnp.sin(angles)
    return (
        jnp.concatenate([cosines, cosines], axis=1),
        jnp.concatenate([-sines, sines], axis=1),
    )


def attention_kernel(
    per_group, ratio, numbers, query, key, value, cosines, sines, block, out, rotated, top, total, acc
):
    step = pl.program_id(0)
    scale = HD**-0.5 * LOG2E
    length = numbers[per_group]
    slots = query.shape[0]
    across = (((1,), (1,)), ((), ()))

    @pl.when(step == 0)
    def _():
        rows = lax.broadcasted_iota(jnp.int32, (slots, slots), 0)
        cols = lax.broadcasted_iota(jnp.int32, (slots, slots), 1)
        visible = (cols <= rows) & (cols < length)
        for r in range(ratio):
            head = query[:, r * HD : (r + 1) * HD].astype(jnp.float32)
            turned = pltpu.roll(head, HD // 2, 1)
            q = (head * cosines[...] + turned * sines[...]).astype(jnp.bfloat16)
            rotated[r] = q
            s = lax.dot_general(q, key[...], across, preferred_element_type=jnp.float32)
            s = jnp.where(visible, s, NEGATIVE)
            m = jnp.max(s, axis=1, keepdims=True)
            p = jnp.exp2((s - m) * scale)
            top[r] = jnp.broadcast_to(m, (slots, HD))
            total[r] = jnp.broadcast_to(jnp.sum(p, axis=1, keepdims=True), (slots, HD))
            acc[r] = jnp.dot(
                p.astype(jnp.bfloat16), value[...], preferred_element_type=jnp.float32
            )

    keys = block[0, :, :HD]
    values = block[0, :, HD:]
    for r in range(ratio):
        s = lax.dot_general(rotated[r], keys, across, preferred_element_type=jnp.float32)
        before = top[r][:, :1]
        m = jnp.maximum(before, jnp.max(s, axis=1, keepdims=True))
        keep = jnp.exp2((before - m) * scale)
        p = jnp.exp2((s - m) * scale)
        top[r] = jnp.broadcast_to(m, (slots, HD))
        total[r] = total[r] * keep + jnp.sum(p, axis=1, keepdims=True)
        acc[r] = acc[r] * keep + jnp.dot(
            p.astype(jnp.bfloat16), values, preferred_element_type=jnp.float32
        )

    @pl.when(step == per_group - 1)
    def _():
        live = lax.broadcasted_iota(jnp.int32, (slots, HD), 0) < length
        for r in range(ratio):
            o = jnp.where(live, acc[r] / total[r], 0.0)
            out[:, r * HD : (r + 1) * HD] = o.astype(jnp.bfloat16)


def attention(head, numbers, query, key, value, cosines, sines, gathered, ratio):
    slots = query.shape[0]
    per_group = numbers.shape[0] - 1
    pblk = gathered.shape[1]
    width = ratio * HD
    fixed = lambda j: (lambda b, n: (0, j))
    return pl.pallas_call(
        functools.partial(attention_kernel, per_group, ratio),
        out_shape=jax.ShapeDtypeStruct((slots, width), jnp.bfloat16),
        grid_spec=pltpu.PrefetchScalarGridSpec(
            num_scalar_prefetch=1,
            grid=(per_group,),
            in_specs=[
                pl.BlockSpec((slots, width), fixed(head)),
                pl.BlockSpec((slots, HD), fixed(head)),
                pl.BlockSpec((slots, HD), fixed(head)),
                pl.BlockSpec((slots, HD), fixed(0)),
                pl.BlockSpec((slots, HD), fixed(0)),
                pl.BlockSpec((1, pblk, 2 * HD), lambda b, n: (n[b], 0, 0)),
            ],
            out_specs=pl.BlockSpec((slots, width), fixed(0)),
            scratch_shapes=[
                pltpu.VMEM((ratio, slots, HD), jnp.bfloat16),
                pltpu.VMEM((ratio, slots, HD), jnp.float32),
                pltpu.VMEM((ratio, slots, HD), jnp.float32),
                pltpu.VMEM((ratio, slots, HD), jnp.float32),
            ],
        ),
        compiler_params=pltpu.CompilerParams(vmem_limit_bytes=32 * 1024 * 1024),
        cost_estimate=pl.CostEstimate(
            flops=4 * slots * width * pblk * per_group * 4,
            bytes_accessed=per_group * pblk * 2 * HD * 2 + 2 * slots * width * 2,
            transcendentals=slots * ratio * pblk * per_group,
        ),
    )(numbers, query, key, value, cosines, sines, gathered)


def shards(
    suffix_query,
    suffix_key,
    suffix_value,
    prefix_key,
    prefix_value,
    residual,
    out_weight,
    norm_gain,
    lengths,
    request_slot,
    prefix_owner,
    request_group,
):
    slots = suffix_query.shape[0]
    kv_heads = suffix_key.shape[1] // HD
    ratio = suffix_query.shape[1] // HD // kv_heads
    devices = lax.axis_size("req")
    sides = lax.axis_size("tp")
    side = lax.axis_index("tp")
    per_group = devices // GROUPS
    prefix_length = prefix_key.shape[1] * per_group
    width_total = residual.shape[1]
    columns = width_total // sides
    chunk = ratio * HD
    first_last = (kv_heads - 1) * chunk

    def send(array, shift):
        return lax.ppermute(array, "tp", [(i, (i + shift) % sides) for i in range(sides)])

    def columns_of(array, shift):
        start = lax.rem(side + shift, sides) * columns
        return lax.dynamic_slice_in_dim(array, start, columns, 1)

    gathered = []
    for head in range(kv_heads):
        cut = slice(head * HD, (head + 1) * HD)
        both = jnp.concatenate([prefix_key[:, :, cut], prefix_value[:, :, cut]], axis=2)
        if gathered:
            both, gathered[-1] = lax.optimization_barrier((both, gathered[-1]))
        gathered.append(lax.all_gather(both, "req", axis=0, tiled=True))

    last_rows = out_weight[first_last:]
    weights_in = [send(columns_of(last_rows, shift), shift) for shift in range(1, sides)]

    request = request_slot[lax.axis_index("req")]
    group_here = request_group[request, 0]
    length_here = lengths[request]
    holders = lax.dynamic_slice_in_dim(prefix_owner, group_here * per_group, per_group)
    numbers = jnp.concatenate([holders, length_here[None]]).astype(jnp.int32)

    cosines, sines = rope_tables(slots, prefix_length)
    per_head = suffix_key.astype(jnp.float32).reshape(slots, kv_heads, HD)
    turned = jnp.concatenate([per_head[..., HD // 2 :], per_head[..., : HD // 2]], axis=-1)
    keys_rot = per_head * cosines[:, None, :] + turned * sines[:, None, :]
    live_rows = jnp.arange(slots, dtype=jnp.int32) < length_here
    cache_key = (
        jnp.where(live_rows[:, None, None], keys_rot, 0.0)
        .astype(jnp.bfloat16)
        .reshape(slots, kv_heads * HD)
    )

    attn = []
    for head in range(kv_heads):
        attn.append(
            attention(
                head, numbers, suffix_query, cache_key, suffix_value, cosines, sines,
                gathered[head], ratio,
            )
        )

    own = columns_of(residual, 0).astype(jnp.float32)
    projected = None
    for head in range(kv_heads - 1):
        term = jnp.dot(
            attn[head],
            out_weight[head * chunk : (head + 1) * chunk],
            preferred_element_type=jnp.float32,
        )
        projected = term if projected is None else projected + term
    if projected is not None:
        own = own + columns_of(projected, 0)
        for shift in range(1, sides):
            part = columns_of(projected, shift).astype(jnp.bfloat16)
            own = own + send(part, shift).astype(jnp.float32)
    last_in = [send(attn[-1], shift) for shift in range(1, sides)]
    own = own + jnp.dot(attn[-1], columns_of(last_rows, 0), preferred_element_type=jnp.float32)
    for last, weight in zip(last_in, weights_in):
        own = own + jnp.dot(last, weight, preferred_element_type=jnp.float32)

    hidden = own.astype(jnp.bfloat16)
    widened = hidden.astype(jnp.float32)
    mine = jnp.sum(widened * widened, axis=1)
    row_squares = mine
    for shift in range(1, sides):
        row_squares = row_squares + send(mine, shift)
    scale_rows = lax.rsqrt(row_squares / width_total + EPSILON)
    normed = (widened * scale_rows[:, None] * norm_gain.astype(jnp.float32)[None, :]).astype(
        jnp.bfloat16
    )
    return (hidden, normed, cache_key)


def solution(mesh):
    return jax.shard_map(
        shards,
        mesh=mesh,
        in_specs=(
            P("req", "tp"),
            P("req", "tp"),
            P("req", "tp"),
            P("req", None, "tp"),
            P("req", None, "tp"),
            P("req", None),
            P("tp", None),
            P("tp"),
            P(),
            P(),
            P(),
            P(),
        ),
        out_specs=(P("req", "tp"), P("req", "tp"), P("req", "tp")),
        check_vma=False,
    )
```

```python
import functools

import jax
import jax.numpy as jnp
from jax import lax
from jax.experimental import pallas as pl
from jax.experimental.pallas import tpu as pltpu
from jax.sharding import PartitionSpec as P

HD = 128
GROUPS = 4

THETA = 1000000.0
NEGATIVE = -1e30
EPSILON = 1e-06
LOG2E = 1.4426950408889634


def rope_tables(row_count, position_base):
    half_dim = HD // 2
    positions = (position_base + jnp.arange(row_count)).astype(jnp.float32)
    frequency = THETA ** (-(jnp.arange(half_dim).astype(jnp.float32) * 2.0 / HD))
    angles = positions[:, None] * frequency[None, :]
    cosines, sines = jnp.cos(angles), jnp.sin(angles)
    return (
        jnp.concatenate([cosines, cosines], axis=1),
        jnp.concatenate([-sines, sines], axis=1),
    )


def attention_kernel(
    per_group, ratio, numbers, query, key, value, cosines, sines, block, out, rotated, top, total, acc
):
    step = pl.program_id(0)
    scale = HD**-0.5 * LOG2E
    length = numbers[per_group]
    slots = query.shape[0]
    across = (((1,), (1,)), ((), ()))

    @pl.when(step == 0)
    def _():
        rows = lax.broadcasted_iota(jnp.int32, (slots, slots), 0)
        cols = lax.broadcasted_iota(jnp.int32, (slots, slots), 1)
        visible = (cols <= rows) & (cols < length)
        for r in range(ratio):
            head = query[:, r * HD : (r + 1) * HD].astype(jnp.float32)
            turned = pltpu.roll(head, HD // 2, 1)
            q = (head * cosines[...] + turned * sines[...]).astype(jnp.bfloat16)
            rotated[r] = q
            s = lax.dot_general(q, key[...], across, preferred_element_type=jnp.float32)
            s = jnp.where(visible, s, NEGATIVE)
            m = jnp.max(s, axis=1, keepdims=True)
            p = jnp.exp2((s - m) * scale)
            top[r] = jnp.broadcast_to(m, (slots, HD))
            total[r] = jnp.broadcast_to(jnp.sum(p, axis=1, keepdims=True), (slots, HD))
            acc[r] = jnp.dot(
                p.astype(jnp.bfloat16), value[...], preferred_element_type=jnp.float32
            )

    keys = block[0, :, :HD]
    values = block[0, :, HD:]
    for r in range(ratio):
        s = lax.dot_general(rotated[r], keys, across, preferred_element_type=jnp.float32)
        before = top[r][:, :1]
        m = jnp.maximum(before, jnp.max(s, axis=1, keepdims=True))
        keep = jnp.exp2((before - m) * scale)
        p = jnp.exp2((s - m) * scale)
        top[r] = jnp.broadcast_to(m, (slots, HD))
        total[r] = total[r] * keep + jnp.sum(p, axis=1, keepdims=True)
        acc[r] = acc[r] * keep + jnp.dot(
            p.astype(jnp.bfloat16), values, preferred_element_type=jnp.float32
        )

    @pl.when(step == per_group - 1)
    def _():
        live = lax.broadcasted_iota(jnp.int32, (slots, HD), 0) < length
        for r in range(ratio):
            o = jnp.where(live, acc[r] / total[r], 0.0)
            out[:, r * HD : (r + 1) * HD] = o.astype(jnp.bfloat16)


def attention(head, numbers, query, key, value, cosines, sines, gathered, place, ratio):
    slots = query.shape[0]
    per_group = numbers.shape[0] - 1
    pblk = gathered.shape[1]
    width = ratio * HD
    fixed = lambda j: (lambda b, n: (0, j))
    return pl.pallas_call(
        functools.partial(attention_kernel, per_group, ratio),
        out_shape=jax.ShapeDtypeStruct((slots, width), jnp.bfloat16),
        grid_spec=pltpu.PrefetchScalarGridSpec(
            num_scalar_prefetch=1,
            grid=(per_group,),
            in_specs=[
                pl.BlockSpec((slots, width), fixed(head)),
                pl.BlockSpec((slots, HD), fixed(head)),
                pl.BlockSpec((slots, HD), fixed(head)),
                pl.BlockSpec((slots, HD), fixed(0)),
                pl.BlockSpec((slots, HD), fixed(0)),
                pl.BlockSpec((1, pblk, 2 * HD), lambda b, n: (n[b], 0, place)),
            ],
            out_specs=pl.BlockSpec((slots, width), fixed(0)),
            scratch_shapes=[
                pltpu.VMEM((ratio, slots, HD), jnp.bfloat16),
                pltpu.VMEM((ratio, slots, HD), jnp.float32),
                pltpu.VMEM((ratio, slots, HD), jnp.float32),
                pltpu.VMEM((ratio, slots, HD), jnp.float32),
            ],
        ),
        compiler_params=pltpu.CompilerParams(vmem_limit_bytes=56 * 1024 * 1024),
        cost_estimate=pl.CostEstimate(
            flops=4 * slots * width * pblk * per_group * 4,
            bytes_accessed=per_group * pblk * 2 * HD * 2 + 2 * slots * width * 2,
            transcendentals=slots * ratio * pblk * per_group,
        ),
    )(numbers, query, key, value, cosines, sines, gathered)


def shards(
    suffix_query,
    suffix_key,
    suffix_value,
    prefix_key,
    prefix_value,
    residual,
    out_weight,
    norm_gain,
    lengths,
    request_slot,
    prefix_owner,
    request_group,
):
    slots = suffix_query.shape[0]
    kv_heads = suffix_key.shape[1] // HD
    ratio = suffix_query.shape[1] // HD // kv_heads
    devices = lax.axis_size("req")
    sides = lax.axis_size("tp")
    side = lax.axis_index("tp")
    per_group = devices // GROUPS
    prefix_length = prefix_key.shape[1] * per_group
    width_total = residual.shape[1]
    columns = width_total // sides
    chunk = ratio * HD
    first_last = (kv_heads - 1) * chunk

    def send(array, shift):
        return lax.ppermute(array, "tp", [(i, (i + shift) % sides) for i in range(sides)])

    def columns_of(array, shift):
        start = lax.rem(side + shift, sides) * columns
        return lax.dynamic_slice_in_dim(array, start, columns, 1)

    def last_columns(shift):
        start = lax.rem(side + shift, sides) * columns
        return lax.dynamic_slice(out_weight, (first_last, start), (chunk, columns))

    def pair(head):
        cut = slice(head * HD, (head + 1) * HD)
        return jnp.concatenate([prefix_key[:, :, cut], prefix_value[:, :, cut]], axis=2)

    request = request_slot[lax.axis_index("req")]
    group_here = request_group[request, 0]
    length_here = lengths[request]
    holders = lax.dynamic_slice_in_dim(prefix_owner, group_here * per_group, per_group)
    numbers = jnp.concatenate([holders, length_here[None]]).astype(jnp.int32)

    cosines, sines = rope_tables(slots, prefix_length)
    per_head = suffix_key.astype(jnp.float32).reshape(slots, kv_heads, HD)
    turned = jnp.concatenate([per_head[..., HD // 2 :], per_head[..., : HD // 2]], axis=-1)
    keys_rot = per_head * cosines[:, None, :] + turned * sines[:, None, :]
    live_rows = jnp.arange(slots, dtype=jnp.int32) < length_here
    cache_key = (
        jnp.where(live_rows[:, None, None], keys_rot, 0.0)
        .astype(jnp.bfloat16)
        .reshape(slots, kv_heads * HD)
    )

    last_out = [last_columns(shift) for shift in range(1, sides)]
    last_pair = pair(kv_heads - 1)
    sources = []
    if kv_heads > 1:
        first = jnp.concatenate([pair(head) for head in range(kv_heads - 1)], axis=2)
        first = lax.all_gather(first, "req", axis=0, tiled=True)
        first, last_pair, numbers, cache_key, cosines, sines, last_out = lax.optimization_barrier(
            (first, last_pair, numbers, cache_key, cosines, sines, last_out)
        )
        sources = [(first, head) for head in range(kv_heads - 1)]
    sources.append((lax.all_gather(last_pair, "req", axis=0, tiled=True), 0))
    weights_in = [send(last_out[shift - 1], shift) for shift in range(1, sides)]

    attn = []
    for head in range(kv_heads):
        attn.append(
            attention(
                head, numbers, suffix_query, cache_key, suffix_value, cosines, sines,
                *sources[head], ratio,
            )
        )

    own = columns_of(residual, 0).astype(jnp.float32)
    projected = None
    for head in range(kv_heads - 1):
        term = jnp.dot(
            attn[head],
            out_weight[head * chunk : (head + 1) * chunk],
            preferred_element_type=jnp.float32,
        )
        projected = term if projected is None else projected + term
    if projected is not None:
        own = own + columns_of(projected, 0)
        for shift in range(1, sides):
            part = columns_of(projected, shift).astype(jnp.bfloat16)
            own = own + send(part, shift).astype(jnp.float32)
    last_in = [send(attn[-1], shift) for shift in range(1, sides)]
    own = own + jnp.dot(attn[-1], last_columns(0), preferred_element_type=jnp.float32)
    for last, weight in zip(last_in, weights_in):
        own = own + jnp.dot(last, weight, preferred_element_type=jnp.float32)

    hidden = own.astype(jnp.bfloat16)
    widened = hidden.astype(jnp.float32)
    mine = jnp.sum(widened * widened, axis=1)
    row_squares = mine
    for shift in range(1, sides):
        row_squares = row_squares + send(mine, shift)
    scale_rows = lax.rsqrt(row_squares / width_total + EPSILON)
    normed = (widened * scale_rows[:, None] * norm_gain.astype(jnp.float32)[None, :]).astype(
        jnp.bfloat16
    )
    return (hidden, normed, cache_key)


def solution(mesh):
    return jax.shard_map(
        shards,
        mesh=mesh,
        in_specs=(
            P("req", "tp"),
            P("req", "tp"),
            P("req", "tp"),
            P("req", None, "tp"),
            P("req", None, "tp"),
            P("req", None),
            P("tp", None),
            P("tp"),
            P(),
            P(),
            P(),
            P(),
        ),
        out_specs=(P("req", "tp"), P("req", "tp"), P("req", "tp")),
        check_vma=False,
    )
```
